32 devices in a mesh: groups: 1, wide: 8 (over z, core), narrow: 4 (over y, x).
Axes of the slice: x: 2, y: 2, z: 4, core: 2. Of those that a mesh axis runs over, the one named last changes fastest.
Arguments:
- tokens: bfloat16 [256, 8192], P(('groups', 'narrow'), 'wide'), may hold values from -6 to 6
- norm_gain: bfloat16 [8192], P('wide'), may hold values from 0.099609375 to 1.8984375
- gate_blocks: bfloat16 [256, 80, 4096], P(('wide', 'narrow')), may hold values from -0.09375 to 0.09375
- gate_ids: int32 [256, 80], P(('wide', 'narrow')), may hold values from -1 to 127, as said below
- up_blocks: bfloat16 [256, 80, 4096], P(('wide', 'narrow')), may hold values from -0.09375 to 0.09375
- up_ids: int32 [256, 80], P(('wide', 'narrow')), may hold values from -1 to 127, as said below
- down_blocks: bfloat16 [256, 80, 4096], P(('wide', 'narrow')), may hold values from -0.0625 to 0.0625
- down_ids: int32 [256, 80], P(('wide', 'narrow')), may hold values from -1 to 127, as said below
Outputs:
- layer_output: bfloat16 [256, 8192], P(('groups', 'narrow'), 'wide')
The draws below stay inside these ranges and needn't reach their ends.
Inputs may be any that keep to these rules, and one draw needn't show every extreme that they name: `gate_ids`: each row lists distinct width blocks in its first slots and -1 in the rest; every row lists between 48 and 80 blocks, and some row lists exactly 80. `up_ids`: as for gate_ids. `down_ids`: as for gate_ids.
All inputs are finite; a program needn't handle non-finite values.
Results may differ from the reference program's by a relative error of at most 0.0064.
Values may be sent and summed in bfloat16 or wider, within the bound.
A program may use at most 256 MiB of HBM per device.

```python
import jax
import jax.numpy as jnp
from jax import lax

D = 8192
FF = 16384
BLOCK = 64
KMAX = 80
TOKENS = 256
FF_BLOCKS = 256


def draw_lists(key):
    width_blocks = D // BLOCK
    columns = FF // BLOCK
    count_key, ranking_key, pick_key = jax.random.split(key, 3)
    counts = jax.random.randint(count_key, (columns,), width_blocks - KMAX, KMAX + 1)
    chosen = jax.random.randint(pick_key, (), 0, columns)
    counts = jnp.where(jnp.arange(columns) == chosen, KMAX, counts)
    scores = jax.random.randint(ranking_key, (columns, width_blocks), 0, 1 << 20) * width_blocks
    scores = scores + jnp.arange(width_blocks)[None, :]
    ranking = jnp.argsort(scores, axis=1)[:, :KMAX]
    present = jnp.arange(KMAX)[None, :] < counts[:, None]
    return jnp.where(present, ranking, -1).astype(jnp.int32)


def draw_gate_ids(key, part):
    key = jax.random.fold_in(key, 11)
    return draw_lists(key)


def draw_up_ids(key, part):
    key = jax.random.fold_in(key, 12)
    return draw_lists(key)


def draw_down_ids(key, part):
    key = jax.random.fold_in(key, 13)
    return draw_lists(key)


def steps_of(own_key, dims, cuts, smallest, high):
    def one(dim, blocks):
        steps = jax.random.uniform(jax.random.fold_in(jax.random.fold_in(own_key, 6), dim), (blocks,), jnp.float32, smallest / len(cuts), high / len(cuts))
        return jnp.repeat(jnp.exp(steps), dims[dim] // blocks).reshape((-1,) + (1,) * (len(dims) - dim - 1))

    level = one(*cuts[0])
    for cut in cuts[1:]:
        level = level * one(*cut)
    return level


def gaussian(own_key, dims, scale, reach, shards=(), kind=jnp.bfloat16):
    loudness = steps_of(own_key, dims, shards, -0.22, 0.18) if shards else 1.0
    array = jax.random.normal(own_key, dims, jnp.float32) * scale * loudness
    return jnp.minimum(jnp.maximum(array, -reach), reach).astype(kind)


def setup_inputs(seed: int = 0, part: int = 0) -> dict:
    streams_of = jax.random.split(jax.random.key(seed), 9)
    part_keys = jax.random.split(jax.random.fold_in(streams_of[8], part), 9)
    tokens = gaussian(part_keys[0], (TOKENS, D), 1.0, 6.0, ((0, 4), (1, 8)))
    norm_gain = jnp.clip(1.0 + 0.18 * jax.random.normal(streams_of[1], (D,), jnp.float32), 0.099609375, 1.8984375).astype(jnp.bfloat16)
    gate_blocks = gaussian(streams_of[2], (FF_BLOCKS, KMAX, BLOCK * BLOCK), (D // 2) ** -0.5, 0.09375, ((0, 32),))
    gate_ids = draw_gate_ids(jax.random.fold_in(streams_of[8], 71), part)
    up_blocks = gaussian(streams_of[4], (FF_BLOCKS, KMAX, BLOCK * BLOCK), (D // 2) ** -0.5, 0.09375, ((0, 32),))
    up_ids = draw_up_ids(jax.random.fold_in(streams_of[8], 71), part)
    down_blocks = gaussian(streams_of[6], (FF_BLOCKS, KMAX, BLOCK * BLOCK), (FF // 2) ** -0.5, 0.0625, ((0, 32),))
    down_ids = draw_down_ids(jax.random.fold_in(streams_of[8], 71), part)
    return {"tokens": tokens, "norm_gain": norm_gain, "gate_blocks": gate_blocks, "gate_ids": gate_ids, "up_blocks": up_blocks, "up_ids": up_ids, "down_blocks": down_blocks, "down_ids": down_ids}


def rms_normed(tokens, norm_gain):
    values = tokens.astype(jnp.float32)
    inverse_rms = lax.rsqrt(lax.optimization_barrier(jnp.mean(values * values, axis=-1, keepdims=True)) + 1e-05)
    return (values * inverse_rms * norm_gain.astype(jnp.float32)).astype(jnp.bfloat16)

def reference(tokens, norm_gain, gate_blocks, gate_ids, up_blocks, up_ids, down_blocks, down_ids):
    normed = rms_normed(tokens, norm_gain)
    row_count = normed.shape[0]
    pieces = normed.astype(jnp.float32).reshape(row_count, D // BLOCK, BLOCK)

    def project_in(weights, block_list):
        present = block_list >= 0
        picked = jnp.take(pieces, jnp.maximum(block_list, 0).astype(jnp.int32), axis=1)
        picked = picked.reshape(row_count, KMAX * BLOCK)
        masked = jnp.where(present[:, None], weights, jnp.zeros_like(weights)).astype(jnp.float32)
        return jnp.dot(picked, masked.reshape(KMAX * BLOCK, BLOCK), preferred_element_type=jnp.float32)

    def advance(running, blocks_now):
        gate_part, gate_list, up_part, up_list, down_part, down_list = blocks_now
        hidden = (jax.nn.silu(project_in(gate_part, gate_list)) * project_in(up_part, up_list)).astype(jnp.bfloat16)
        hidden = lax.optimization_barrier(hidden).astype(jnp.float32)
        present = down_list >= 0
        masked = jnp.where(present[:, None], down_part, jnp.zeros_like(down_part)).astype(jnp.float32)
        masked = masked.reshape(KMAX, BLOCK, BLOCK)
        contributions = jnp.einsum('ri,kij->krj', hidden, masked)
        summed = jax.ops.segment_sum(contributions, jnp.maximum(down_list, 0).astype(jnp.int32), num_segments=D // BLOCK)
        return (running + summed, None)
    start = jnp.zeros((D // BLOCK, row_count, BLOCK), jnp.float32)
    running, _ = lax.scan(advance, start, (gate_blocks, gate_ids, up_blocks, up_ids, down_blocks, down_ids))
    return running.transpose(1, 0, 2).reshape(row_count, D).astype(jnp.bfloat16)
```

```python
import functools

import jax
import jax.numpy as jnp
from jax import lax
from jax.experimental import pallas as pl
from jax.experimental.pallas import tpu as pltpu
from jax.sharding import PartitionSpec as P

BLOCK = 64
BF = jnp.bfloat16
F32 = jnp.float32


def normalize(gathered, gain_all):
    values = gathered.astype(jnp.float32)
    inverse_rms = lax.rsqrt(jnp.mean(values * values, axis=-1, keepdims=True) + 1e-05)
    return (values * inverse_rms * gain_all.astype(jnp.float32)).astype(jnp.bfloat16)


def project_in(normed, part, block_list):
    row_count, width_total = normed.shape
    count_blocks, slot_count = block_list.shape
    pieces = normed.reshape(row_count, width_total // BLOCK, BLOCK)
    picked = jnp.take(pieces, jnp.maximum(block_list, 0).reshape(-1), axis=1)
    picked = picked.reshape(row_count, count_blocks, slot_count, BLOCK)
    tiles = jnp.where((block_list >= 0)[:, :, None], part, jnp.zeros_like(part))
    tiles = tiles.reshape(count_blocks, slot_count, BLOCK, BLOCK)
    result = jnp.einsum("rfkc,fkcj->rfj", picked, tiles, preferred_element_type=jnp.float32)
    return result.reshape(row_count, count_blocks * BLOCK)


def dense_down(part, block_list, width_total):
    count_blocks, slot_count = block_list.shape
    width_blocks = width_total // BLOCK
    selector = jax.nn.one_hot(block_list, width_blocks, dtype=jnp.bfloat16)
    tiles = part.reshape(count_blocks, slot_count, BLOCK, BLOCK)
    placed = jnp.einsum("fkb,fkij->fibj", selector, tiles, preferred_element_type=jnp.bfloat16)
    return placed.reshape(count_blocks * BLOCK, width_total)


def gated_hidden(normed, gate_part, gate_list, up_part, up_list):
    gate_value = project_in(normed, gate_part, gate_list)
    upward = project_in(normed, up_part, up_list)
    return (jax.nn.silu(gate_value) * upward).astype(jnp.bfloat16)


def plain(tokens, norm_gain, gate_blocks, gate_ids, up_blocks, up_ids, down_blocks, down_ids):
    gathered, gain_all = (
        lax.all_gather(tokens, "wide", axis=1, tiled=True),
        lax.all_gather(norm_gain, "wide", axis=0, tiled=True),
    )
    normed = normalize(gathered, gain_all)
    group_normed = lax.all_gather(normed, "narrow", axis=0, tiled=True)
    local_hidden = gated_hidden(group_normed, gate_blocks, gate_ids, up_blocks, up_ids)
    hidden = lax.all_to_all(local_hidden, "narrow", split_axis=0, concat_axis=1, tiled=True)
    down_all, down_list = (
        lax.all_gather(down_blocks, "narrow", axis=0, tiled=True),
        lax.all_gather(down_ids, "narrow", axis=0, tiled=True),
    )
    panel_dense = dense_down(down_all, down_list, gathered.shape[1])
    partial_value = jnp.dot(hidden, panel_dense, preferred_element_type=jnp.float32)
    return lax.psum_scatter(partial_value, "wide", scatter_dimension=1, tiled=True).astype(
        jnp.bfloat16
    )


def one_hot(rows, columns, source_of):
    r = lax.broadcasted_iota(jnp.int32, (rows, columns), 0)
    d = lax.broadcasted_iota(jnp.int32, (rows, columns), 1)
    return jnp.where(r == source_of(d), 1.0, 0.0).astype(BF)


def low_half(rows):
    return lax.broadcasted_iota(jnp.int32, (rows, 128), 1) < 64


def swap(x):
    return pltpu.roll(x, 64, 1)


class Panels:
    def __init__(self, blocks, ids, raw, sel, turn, in_w, down_w, sems):
        self.blocks, self.ids, self.raw, self.sel, self.turn = blocks, ids, raw, sel, turn
        self.in_w, self.down_w, self.sems = in_w, down_w, sems
        self.pairs = blocks[0].shape[0] // 2
        self.slots = blocks[0].shape[1]
        self.steps = [(k, q) for k in range(3) for q in range(self.pairs)]

    def copies(self, n):
        kind, q = self.steps[n]
        return [
            pltpu.make_async_copy(
                self.blocks[kind].at[2 * q + e],
                self.raw.at[n % 2, pl.ds(128 * e, self.slots)],
                self.sems.at[n % 2, e],
            )
            for e in range(2)
        ]

    def begin(self):
        self.raw[...] = jnp.zeros_like(self.raw)
        self.sel[...] = jnp.zeros_like(self.sel)
        for c in self.copies(0):
            c.start()

    def step(self, n):
        kind, q = self.steps[n]
        if n + 1 < len(self.steps):
            for c in self.copies(n + 1):
                c.start()
        row = lax.broadcasted_iota(jnp.int32, (128, self.slots), 0)
        if kind == 2:
            row = 2 * (row % 64) + row // 64
        for e in range(2):
            hit = self.ids[kind][2 * q + e : 2 * q + e + 1, :] == row
            self.sel[128 * e : 128 * e + 128, 128 * e : 128 * e + self.slots] = jnp.where(hit, 1.0, 0.0).astype(BF)
        for c in self.copies(n):
            c.wait()
        if kind < 2:
            self.place_in(n % 2, (kind * self.pairs + q) * 128)
        else:
            self.place_down(n % 2, q)

    def picked(self, slot, c):
        lanes = pl.ds(pl.multiple_of(c * 256, 256), 256)
        return jnp.dot(self.sel[...], self.raw[slot, :, lanes], preferred_element_type=F32)

    def place_in(self, slot, column):
        low = low_half(128)

        def body(c, carry):
            s = self.picked(slot, c)
            for k in range(2):
                a = s[:128, 128 * k : 128 * k + 128]
                b = swap(s[128:, 128 * k : 128 * k + 128])
                at = pl.ds(pl.multiple_of((2 * c + k) * 16, 16), 16)
                for p, v in enumerate((jnp.where(low, a, b), jnp.where(low, b, a))):
                    self.in_w[p, :, at, column : column + 128] = v.astype(BF).reshape(8, 16, 128)
            return carry

        lax.fori_loop(0, 16, body, 0)

    def place_down(self, slot, q):
        low = low_half(64)

        def body(c, carry):
            s = self.picked(slot, c)
            for k in range(2):
                for e in range(2):
                    a = s[128 * e : 128 * e + 64, 128 * k : 128 * k + 128]
                    b = s[128 * e + 64 : 128 * e + 128, 128 * k : 128 * k + 128]
                    at = pl.ds(2 * c + k, 64, stride=32)
                    self.turn[2 * e, at, :] = jnp.where(low, a, swap(b))
                    self.turn[2 * e + 1, at, :] = jnp.where(low, swap(a), b)
            return carry

        lax.fori_loop(0, 16, body, 0)
        for e in range(2):
            for p in range(2):
                first = p * 64 * self.pairs + (2 * q + e) * 32
                for b in range(64):
                    self.down_w[first : first + 32, 128 * b : 128 * b + 128] = self.turn[
                        2 * e + p, 32 * b : 32 * b + 32, :
                    ].astype(BF)


def gather_product(x_ref, in_w, acc, w, first):
    for p in range(2):
        term = jnp.dot(x_ref[w, :, 512 * p : 512 * p + 512], in_w[p, w], preferred_element_type=F32)
        if first:
            acc[p] = term
        else:
            acc[p] += term


def hidden_of(acc, half):
    cols = []
    for t in range(2 * half // 128):
        at = slice(128 * t, 128 * t + 128)
        cols.append(acc[0, :, at] + swap(acc[1, :, at]))
    count = half // 128
    out = [(jax.nn.silu(cols[t]) * cols[count + t]).astype(BF) for t in range(count)]
    h = jnp.concatenate(out, axis=1)
    quarter = half // 2

    def source(d):
        return (d % quarter) // 32 * 64 + 2 * (d % 32) + d // quarter

    return jnp.dot(h, one_hot(half, half, source), preferred_element_type=F32).astype(BF)


def compute_kernel(x_ref, gi, ui, di, gb, ub, db, out, raw, sel, turn, in_w, down_w, acc, sems):
    panels = Panels((gb, ub, db), (gi, ui, di), raw, sel, turn, in_w, down_w, sems)
    panels.begin()
    for n in range(len(panels.steps)):
        panels.step(n)
    for w in range(8):
        gather_product(x_ref, in_w, acc, w, w == 0)
    h = hidden_of(acc, in_w.shape[3] // 2)
    for w in range(8):
        out[w] = jnp.dot(h, down_w[:, 1024 * w : 1024 * w + 1024], preferred_element_type=F32)


def compute(x, gate_ids, up_ids, down_ids, gate_blocks, up_blocks, down_blocks):
    count = gate_blocks.shape[0]
    rows = x.shape[1]
    vmem = pl.BlockSpec(memory_space=pltpu.VMEM)
    return pl.pallas_call(
        compute_kernel,
        out_shape=jax.ShapeDtypeStruct(x.shape, F32),
        in_specs=[vmem] * 4 + [pl.BlockSpec(memory_space=pl.ANY)] * 3,
        out_specs=vmem,
        scratch_shapes=[
            pltpu.VMEM((2, 256, 4096), BF),
            pltpu.VMEM((256, 256), BF),
            pltpu.VMEM((4, 2048, 128), F32),
            pltpu.VMEM((2, 8, 512, 128 * count), BF),
            pltpu.VMEM((64 * count, 8192), BF),
            pltpu.VMEM((2, rows, 128 * count), F32),
            pltpu.SemaphoreType.DMA((2, 2)),
        ],
        compiler_params=pltpu.CompilerParams(vmem_limit_bytes=60 * 1024 * 1024),
    )(x, gate_ids, up_ids, down_ids, gate_blocks, up_blocks, down_blocks)


def fused(tokens, norm_gain, gate_blocks, gate_ids, up_blocks, up_ids, down_blocks, down_ids):
    rows, width = tokens.shape
    values = tokens.astype(F32)
    total = lax.psum(jnp.sum(values * values, axis=-1, keepdims=True), "wide")
    normed = (values * lax.rsqrt(total / 8192.0 + 1e-05) * norm_gain.astype(F32)).astype(BF)
    turned = normed.reshape(rows, width // 64, 32, 2).transpose(0, 3, 2, 1).reshape(rows, width)
    x = lax.all_gather(turned, ("wide", "narrow"), axis=0, tiled=False).reshape(8, 4 * rows, width)
    part = compute(x, gate_ids, up_ids, down_ids, gate_blocks, up_blocks, down_blocks)
    part = part.reshape(32 * rows, width)
    return lax.psum_scatter(part, ("wide", "narrow"), scatter_dimension=0, tiled=True).astype(BF)


def solution(mesh):
    placed = (
        P(("groups", "narrow"), "wide"),
        P("wide"),
        P(("wide", "narrow"), None, None),
        P(("wide", "narrow"), None),
        P(("wide", "narrow"), None, None),
        P(("wide", "narrow"), None),
        P(("wide", "narrow"), None, None),
        P(("wide", "narrow"), None),
    )
    local = fused if mesh.shape["wide"] == 8 and mesh.shape["narrow"] == 4 else plain
    return jax.shard_map(
        local,
        mesh=mesh,
        in_specs=placed,
        out_specs=P(("groups", "narrow"), "wide"),
        check_vma=False,
    )
```

```python
import functools

import jax
import jax.numpy as jnp
from jax import lax
from jax.experimental import pallas as pl
from jax.experimental.pallas import tpu as pltpu
from jax.sharding import PartitionSpec as P

BLOCK = 64
BF = jnp.bfloat16
F32 = jnp.float32


def normalize(gathered, gain_all):
    values = gathered.astype(jnp.float32)
    inverse_rms = lax.rsqrt(jnp.mean(values * values, axis=-1, keepdims=True) + 1e-05)
    return (values * inverse_rms * gain_all.astype(jnp.float32)).astype(jnp.bfloat16)


def project_in(normed, part, block_list):
    row_count, width_total = normed.shape
    count_blocks, slot_count = block_list.shape
    pieces = normed.reshape(row_count, width_total // BLOCK, BLOCK)
    picked = jnp.take(pieces, jnp.maximum(block_list, 0).reshape(-1), axis=1)
    picked = picked.reshape(row_count, count_blocks, slot_count, BLOCK)
    tiles = jnp.where((block_list >= 0)[:, :, None], part, jnp.zeros_like(part))
    tiles = tiles.reshape(count_blocks, slot_count, BLOCK, BLOCK)
    result = jnp.einsum("rfkc,fkcj->rfj", picked, tiles, preferred_element_type=jnp.float32)
    return result.reshape(row_count, count_blocks * BLOCK)


def dense_down(part, block_list, width_total):
    count_blocks, slot_count = block_list.shape
    width_blocks = width_total // BLOCK
    selector = jax.nn.one_hot(block_list, width_blocks, dtype=jnp.bfloat16)
    tiles = part.reshape(count_blocks, slot_count, BLOCK, BLOCK)
    placed = jnp.einsum("fkb,fkij->fibj", selector, tiles, preferred_element_type=jnp.bfloat16)
    return placed.reshape(count_blocks * BLOCK, width_total)


def gated_hidden(normed, gate_part, gate_list, up_part, up_list):
    gate_value = project_in(normed, gate_part, gate_list)
    upward = project_in(normed, up_part, up_list)
    return (jax.nn.silu(gate_value) * upward).astype(jnp.bfloat16)


def plain(tokens, norm_gain, gate_blocks, gate_ids, up_blocks, up_ids, down_blocks, down_ids):
    gathered, gain_all = (
        lax.all_gather(tokens, "wide", axis=1, tiled=True),
        lax.all_gather(norm_gain, "wide", axis=0, tiled=True),
    )
    normed = normalize(gathered, gain_all)
    group_normed = lax.all_gather(normed, "narrow", axis=0, tiled=True)
    local_hidden = gated_hidden(group_normed, gate_blocks, gate_ids, up_blocks, up_ids)
    hidden = lax.all_to_all(local_hidden, "narrow", split_axis=0, concat_axis=1, tiled=True)
    down_all, down_list = (
        lax.all_gather(down_blocks, "narrow", axis=0, tiled=True),
        lax.all_gather(down_ids, "narrow", axis=0, tiled=True),
    )
    panel_dense = dense_down(down_all, down_list, gathered.shape[1])
    partial_value = jnp.dot(hidden, panel_dense, preferred_element_type=jnp.float32)
    return lax.psum_scatter(partial_value, "wide", scatter_dimension=1, tiled=True).astype(
        jnp.bfloat16
    )


def one_hot(rows, columns, source_of):
    r = lax.broadcasted_iota(jnp.int32, (rows, columns), 0)
    d = lax.broadcasted_iota(jnp.int32, (rows, columns), 1)
    return jnp.where(r == source_of(d), 1.0, 0.0).astype(BF)


def low_half(rows):
    return lax.broadcasted_iota(jnp.int32, (rows, 128), 1) < 64


def swap(x):
    return pltpu.roll(x, 64, 1)


class Panels:
    def __init__(self, blocks, ids, raw, sel, turn, in_w, down_w, sems):
        self.blocks, self.ids, self.raw, self.sel, self.turn = blocks, ids, raw, sel, turn
        self.in_w, self.down_w, self.sems = in_w, down_w, sems
        self.pairs = blocks[0].shape[0] // 2
        self.slots = blocks[0].shape[1]
        self.steps = [(k, q) for k in range(3) for q in range(self.pairs)]

    def copies(self, n):
        kind, q = self.steps[n]
        return [
            pltpu.make_async_copy(
                self.blocks[kind].at[2 * q + e],
                self.raw.at[n % 2, pl.ds(128 * e, self.slots)],
                self.sems.at[n % 2, e],
            )
            for e in range(2)
        ]

    def begin(self):
        self.raw[...] = jnp.zeros_like(self.raw)
        self.sel[...] = jnp.zeros_like(self.sel)
        for c in self.copies(0):
            c.start()

    def step(self, n):
        kind, q = self.steps[n]
        if n + 1 < len(self.steps):
            for c in self.copies(n + 1):
                c.start()
        row = lax.broadcasted_iota(jnp.int32, (128, self.slots), 0)
        if kind == 2:
            row = 2 * (row % 64) + row // 64
        for e in range(2):
            hit = self.ids[kind][2 * q + e : 2 * q + e + 1, :] == row
            self.sel[128 * e : 128 * e + 128, 128 * e : 128 * e + self.slots] = jnp.where(hit, 1.0, 0.0).astype(BF)
        for c in self.copies(n):
            c.wait()
        if kind < 2:
            self.place_in(n % 2, (kind * self.pairs + q) * 128)
        else:
            self.place_down(n % 2, q)

    def picked(self, slot, c):
        lanes = pl.ds(pl.multiple_of(c * 256, 256), 256)
        return jnp.dot(self.sel[...], self.raw[slot, :, lanes], preferred_element_type=F32)

    def place_in(self, slot, column):
        low = low_half(128)

        def body(c, carry):
            s = self.picked(slot, c)
            for k in range(2):
                a = s[:128, 128 * k : 128 * k + 128]
                b = swap(s[128:, 128 * k : 128 * k + 128])
                at = pl.ds(pl.multiple_of((2 * c + k) * 16, 16), 16)
                for p, v in enumerate((jnp.where(low, a, b), jnp.where(low, b, a))):
                    self.in_w[p, :, at, column : column + 128] = v.astype(BF).reshape(8, 16, 128)
            return carry

        lax.fori_loop(0, 16, body, 0)

    def place_down(self, slot, q):
        low = low_half(64)

        def body(c, carry):
            s = self.picked(slot, c)
            for k in range(2):
                for e in range(2):
                    a = s[128 * e : 128 * e + 64, 128 * k : 128 * k + 128]
                    b = s[128 * e + 64 : 128 * e + 128, 128 * k : 128 * k + 128]
                    at = pl.ds(2 * c + k, 64, stride=32)
                    self.turn[2 * e, at, :] = jnp.where(low, a, swap(b))
                    self.turn[2 * e + 1, at, :] = jnp.where(low, swap(a), b)
            return carry

        lax.fori_loop(0, 16, body, 0)
        for e in range(2):
            for p in range(2):
                first = p * 64 * self.pairs + (2 * q + e) * 32
                for b in range(64):
                    self.down_w[first : first + 32, 128 * b : 128 * b + 128] = self.turn[
                        2 * e + p, 32 * b : 32 * b + 32, :
                    ].astype(BF)


def gather_product(x_ref, in_w, acc, w, first):
    for p in range(2):
        term = jnp.dot(x_ref[w, :, 512 * p : 512 * p + 512], in_w[p, w], preferred_element_type=F32)
        if first:
            acc[p] = term
        else:
            acc[p] += term


def hidden_of(acc, half):
    cols = []
    for t in range(2 * half // 128):
        at = slice(128 * t, 128 * t + 128)
        cols.append(acc[0, :, at] + swap(acc[1, :, at]))
    count = half // 128
    out = [(jax.nn.silu(cols[t]) * cols[count + t]).astype(BF) for t in range(count)]
    h = jnp.concatenate(out, axis=1)
    quarter = half // 2

    def source(d):
        return (d % quarter) // 32 * 64 + 2 * (d % 32) + d // quarter

    return jnp.dot(h, one_hot(half, half, source), preferred_element_type=F32).astype(BF)


def fused_kernel(
    tok, gain, gi, ui, di, gb, ub, db, out,
    raw, sel, turn, in_w, down_w, acc, x, ssum, q, own, send0, land0, send1, land1, send2, land2, send3, land3,
    sems, ss_s, ss_r, z_s, z_r, a_s, a_r, b_s, b_r, c_s, c_r, r0_s, r0_r, r1_s, r1_r, r2_s, r2_r, r3_s, r3_r,
):
    wide, narrow = lax.axis_index("wide"), lax.axis_index("narrow")
    z, core = wide // 2, wide % 2
    y, xx = narrow // 2, narrow % 2
    sibling = {"wide": 2 * z + 1 - core}
    beside = ({"narrow": 2 * y + 1 - xx}, {"narrow": 2 * (1 - y) + xx})
    mine, other = (xx, y), (1 - xx, 1 - y)

    def plane(d):
        return (z + d) % 4

    def rows(h, pair, half, count):
        return pl.ds(pl.multiple_of(128 * h + 64 * pair + 32 * half, 32), count)

    def remote(src, dst, s, r, to):
        return pltpu.make_async_remote_copy(
            src_ref=src, dst_ref=dst, send_sem=s, recv_sem=r, device_id=to, device_id_type=pl.DeviceIdType.MESH
        )

    def own_rows(h):
        return rows(h, mine[1 - h], mine[h], 32)

    values = tok[...].astype(F32)
    ssum[0] = jnp.broadcast_to(jnp.sum(values * values, axis=-1, keepdims=True), ssum.shape[1:])

    barrier = pltpu.get_barrier_semaphore()
    peers = [{"wide": (wide + d) % 8} for d in range(1, 8)] + list(beside)
    for peer in peers:
        pl.semaphore_signal(barrier, inc=1, device_id=peer, device_id_type=pl.DeviceIdType.MESH)
    pl.semaphore_wait(barrier, len(peers))

    sums = [remote(ssum.at[0], ssum.at[d], ss_s.at[d], ss_r.at[d], peers[d - 1]) for d in range(1, 8)]
    for c in sums:
        c.start()

    panels = Panels((gb, ub, db), (gi, ui, di), raw, sel, turn, in_w, down_w, sems)
    panels.begin()
    panels.step(0)

    total = jnp.sum(values * values, axis=-1, keepdims=True)
    for d in range(1, 8):
        sums[d - 1].wait_recv()
        total = total + ssum[d, :, 0:1]
    inverse = lax.rsqrt(total / 8192.0 + 1e-05)
    normed = (values * inverse * gain[...].astype(F32)).astype(BF)
    for t in range(8):

        def source(d):
            d = d + 128 * t
            return (d % 16) * 64 + 2 * ((d % 512) // 16) + d // 512

        part = jnp.dot(normed, one_hot(1024, 128, source), preferred_element_type=F32).astype(BF)
        for h in range(2):
            x[wide, own_rows(h), 128 * t : 128 * t + 128] = part[32 * h : 32 * h + 32]

    def held(d):
        return 2 * plane(4 - d) + core

    along = {}
    first = {}
    second = {}
    last = {}
    for d in range(1, 4):
        for h in range(2):
            ref = x.at[wide, own_rows(h)]
            along[d, h] = remote(ref, ref, z_s.at[d, h], z_r.at[d, h], {"wide": 2 * plane(d) + core})
    for d in range(4):
        for h in range(2):
            ref = x.at[held(d), own_rows(h)]
            first[d, h] = remote(ref, ref, a_s.at[d, h], a_r.at[d, h], beside[h])
            ref = x.at[held(d), rows(h, mine[1 - h], 0, 64)]
            second[d, h] = remote(ref, ref, b_s.at[d, h], b_r.at[d, h], beside[1 - h])
        ref = x.at[held(d)]
        last[d] = remote(ref, ref, c_s.at[d], c_r.at[d], sibling)

    def go_first(d):
        for h in range(2):
            if d:
                along[d, h].wait_recv()
            first[d, h].start()

    def go_second(d):
        for h in range(2):
            first[d, h].wait_recv()
            second[d, h].start()

    def go_last(d):
        for h in range(2):
            second[d, h].wait_recv()
        last[d].start()

    for c in along.values():
        c.start()
    go_first(0)
    after = {
        1: [(go_first, 1), (go_second, 0), (go_first, 2), (go_first, 3)],
        2: [(go_second, 1), (go_last, 0)],
        3: [(go_second, 2), (go_last, 1)],
        4: [(go_second, 3), (go_last, 2)],
        5: [(go_last, 3)],
    }
    for n in range(1, len(panels.steps)):
        panels.step(n)
        for act, d in after.get(n, ()):
            act(d)

    for d in range(4):
        gather_product(x, in_w, acc, held(d), d == 0)
    for d in range(4):
        last[d].wait_recv()
        gather_product(x, in_w, acc, held(d) + 1 - 2 * core, False)
    hidden = hidden_of(acc, in_w.shape[3] // 2)

    def product(w):
        columns = pl.ds(pl.multiple_of(1024 * w, 1024), 1024)
        return jnp.dot(hidden, down_w[:, columns], preferred_element_type=F32)

    order = (1, 2, 3, 0)
    hop0, hop1, hop2, hop3 = {}, {}, {}, {}
    for e in order:
        hop0[e] = remote(send0.at[e], land0.at[e], r0_s.at[e], r0_r.at[e], sibling)
        for h in range(2):
            hop1[e, h] = remote(send1.at[e, h], land1.at[e, h], r1_s.at[e, h], r1_r.at[e, h], beside[1 - h])
            hop2[e, h] = remote(send2.at[e, h], land2.at[e, h], r2_s.at[e, h], r2_r.at[e, h], beside[h])
        if e:
            hop3[e] = remote(send3.at[e], land3.at[e], r3_s.at[e], r3_r.at[e], {"wide": 2 * plane(e) + core})
    for e in order:
        send0[e] = product(2 * plane(e) + 1 - core).astype(BF)
        hop0[e].start()
    for e in order:
        q[e] = product(2 * plane(e) + core)

    def go_hop1(e):
        hop0[e].wait_recv()
        for h in range(2):
            at = rows(h, other[1 - h], 0, 64)
            send1[e, h] = (q[e, at] + land0[e, at].astype(F32)).astype(BF)
            hop1[e, h].start()
        for h in range(2):
            at = rows(h, mine[1 - h], 0, 64)
            q[e, at] = q[e, at] + land0[e, at].astype(F32)

    def go_hop2(e):
        for h in range(2):
            hop1[e, h].wait_recv()
            at = rows(h, mine[1 - h], other[h], 32)
            come = pl.ds(pl.multiple_of(32 * other[h], 32), 32)
            send2[e, h] = (q[e, at] + land1[e, h, come].astype(F32)).astype(BF)
            hop2[e, h].start()

    def go_hop3(e):
        for h in range(2):
            hop2[e, h].wait_recv()
            come = pl.ds(pl.multiple_of(32 * mine[h], 32), 32)
            v = q[e, own_rows(h)] + land1[e, h, come].astype(F32) + land2[e, h].astype(F32)
            if e:
                send3[e, 32 * h : 32 * h + 32] = v.astype(BF)
            else:
                own[32 * h : 32 * h + 32] = v
        if e:
            hop3[e].start()

    for k in range(6):
        for lag, act in enumerate((go_hop1, go_hop2, go_hop3)):
            if 0 <= k - lag < 4:
                act(order[k - lag])
    value = own[...]
    for e in (1, 2, 3):
        hop3[e].wait_recv()
        value = value + land3[e].astype(F32)
    out[...] = value.astype(BF)

    for group in (along, first, second, last, hop0, hop1, hop2, hop3):
        for c in group.values():
            c.wait_send()
    for c in sums:
        c.wait_send()


def fused(tokens, norm_gain, gate_blocks, gate_ids, up_blocks, up_ids, down_blocks, down_ids):
    rows, width = tokens.shape
    count = gate_blocks.shape[0]
    vmem = pl.BlockSpec(memory_space=pltpu.VMEM)
    dma = pltpu.SemaphoreType.DMA
    return pl.pallas_call(
        fused_kernel,
        out_shape=jax.ShapeDtypeStruct(tokens.shape, BF),
        in_specs=[vmem] * 5 + [pl.BlockSpec(memory_space=pl.ANY)] * 3,
        out_specs=vmem,
        scratch_shapes=[
            pltpu.VMEM((2, 256, 4096), BF),
            pltpu.VMEM((256, 256), BF),
            pltpu.VMEM((4, 2048, 128), F32),
            pltpu.VMEM((2, 8, 512, 128 * count), BF),
            pltpu.VMEM((64 * count, 8192), BF),
            pltpu.VMEM((2, 256, 128 * count), F32),
            pltpu.VMEM((8, 256, 1024), BF),
            pltpu.VMEM((8, 64, 128), F32),
            pltpu.VMEM((4, 256, 1024), F32),
            pltpu.VMEM((64, 1024), F32),
            pltpu.VMEM((4, 256, 1024), BF),
            pltpu.VMEM((4, 256, 1024), BF),
            pltpu.VMEM((4, 2, 64, 1024), BF),
            pltpu.VMEM((4, 2, 64, 1024), BF),
            pltpu.VMEM((4, 2, 32, 1024), BF),
            pltpu.VMEM((4, 2, 32, 1024), BF),
            pltpu.VMEM((4, 64, 1024), BF),
            pltpu.VMEM((4, 64, 1024), BF),
            dma((2, 2)),
            dma((8,)), dma((8,)),
            dma((4, 2)), dma((4, 2)),
            dma((4, 2)), dma((4, 2)),
            dma((4, 2)), dma((4, 2)),
            dma((4,)), dma((4,)),
            dma((4,)), dma((4,)),
            dma((4, 2)), dma((4, 2)),
            dma((4, 2)), dma((4, 2)),
            dma((4,)), dma((4,)),
        ],
        compiler_params=pltpu.CompilerParams(
            vmem_limit_bytes=62 * 1024 * 1024, collective_id=0, has_side_effects=True
        ),
    )(tokens, norm_gain.reshape(1, width), gate_ids, up_ids, down_ids, gate_blocks, up_blocks, down_blocks)


def solution(mesh):
    placed = (
        P(("groups", "narrow"), "wide"),
        P("wide"),
        P(("wide", "narrow"), None, None),
        P(("wide", "narrow"), None),
        P(("wide", "narrow"), None, None),
        P(("wide", "narrow"), None),
        P(("wide", "narrow"), None, None),
        P(("wide", "narrow"), None),
    )
    local = fused if mesh.shape["wide"] == 8 and mesh.shape["narrow"] == 4 else plain
    return jax.shard_map(
        local,
        mesh=mesh,
        in_specs=placed,
        out_specs=P(("groups", "narrow"), "wide"),
        check_vma=False,
    )
```

```python
import functools

import jax
import jax.numpy as jnp
from jax import lax
from jax.experimental import pallas as pl
from jax.experimental.pallas import tpu as pltpu
from jax.sharding import PartitionSpec as P

BLOCK = 64
STRIDE = 40
BF = jnp.bfloat16
F32 = jnp.float32


def normalize(gathered, gain_all):
    values = gathered.astype(jnp.float32)
    inverse_rms = lax.rsqrt(jnp.mean(values * values, axis=-1, keepdims=True) + 1e-05)
    return (values * inverse_rms * gain_all.astype(jnp.float32)).astype(jnp.bfloat16)


def project_in(normed, part, block_list):
    row_count, width_total = normed.shape
    count_blocks, slot_count = block_list.shape
    pieces = normed.reshape(row_count, width_total // BLOCK, BLOCK)
    picked = jnp.take(pieces, jnp.maximum(block_list, 0).reshape(-1), axis=1)
    picked = picked.reshape(row_count, count_blocks, slot_count, BLOCK)
    tiles = jnp.where((block_list >= 0)[:, :, None], part, jnp.zeros_like(part))
    tiles = tiles.reshape(count_blocks, slot_count, BLOCK, BLOCK)
    result = jnp.einsum("rfkc,fkcj->rfj", picked, tiles, preferred_element_type=jnp.float32)
    return result.reshape(row_count, count_blocks * BLOCK)


def dense_down(part, block_list, width_total):
    count_blocks, slot_count = block_list.shape
    width_blocks = width_total // BLOCK
    selector = jax.nn.one_hot(block_list, width_blocks, dtype=jnp.bfloat16)
    tiles = part.reshape(count_blocks, slot_count, BLOCK, BLOCK)
    placed = jnp.einsum("fkb,fkij->fibj", selector, tiles, preferred_element_type=jnp.bfloat16)
    return placed.reshape(count_blocks * BLOCK, width_total)


def gated_hidden(normed, gate_part, gate_list, up_part, up_list):
    gate_value = project_in(normed, gate_part, gate_list)
    upward = project_in(normed, up_part, up_list)
    return (jax.nn.silu(gate_value) * upward).astype(jnp.bfloat16)


def plain(tokens, norm_gain, gate_blocks, gate_ids, up_blocks, up_ids, down_blocks, down_ids):
    gathered, gain_all = (
        lax.all_gather(tokens, "wide", axis=1, tiled=True),
        lax.all_gather(norm_gain, "wide", axis=0, tiled=True),
    )
    normed = normalize(gathered, gain_all)
    group_normed = lax.all_gather(normed, "narrow", axis=0, tiled=True)
    local_hidden = gated_hidden(group_normed, gate_blocks, gate_ids, up_blocks, up_ids)
    hidden = lax.all_to_all(local_hidden, "narrow", split_axis=0, concat_axis=1, tiled=True)
    down_all, down_list = (
        lax.all_gather(down_blocks, "narrow", axis=0, tiled=True),
        lax.all_gather(down_ids, "narrow", axis=0, tiled=True),
    )
    panel_dense = dense_down(down_all, down_list, gathered.shape[1])
    partial_value = jnp.dot(hidden, panel_dense, preferred_element_type=jnp.float32)
    return lax.psum_scatter(partial_value, "wide", scatter_dimension=1, tiled=True).astype(
        jnp.bfloat16
    )


def one_hot(rows, columns, source_of):
    r = lax.broadcasted_iota(jnp.int32, (rows, columns), 0)
    d = lax.broadcasted_iota(jnp.int32, (rows, columns), 1)
    return jnp.where(r == source_of(d), 1.0, 0.0).astype(BF)


def low_half(rows):
    return lax.broadcasted_iota(jnp.int32, (rows, 128), 1) < 64


def swap(x):
    return pltpu.roll(x, 64, 1)


class Panels:
    def __init__(self, blocks, ids, raw, sel, turn, in_w, down_w, sems):
        self.blocks, self.ids, self.raw, self.sel, self.turn = blocks, ids, raw, sel, turn
        self.in_w, self.down_w, self.sems = in_w, down_w, sems
        self.pairs = blocks[0].shape[0] // 2
        self.slots = blocks[0].shape[1]
        self.steps = [(k, q) for k in range(3) for q in range(self.pairs)]

    def copies(self, n):
        kind, q = self.steps[n]
        return [
            pltpu.make_async_copy(
                self.blocks[kind].at[2 * q + e],
                self.raw.at[n % 2, pl.ds(128 * e, self.slots)],
                self.sems.at[n % 2, e],
            )
            for e in range(2)
        ]

    def begin(self):
        self.raw[...] = jnp.zeros_like(self.raw)
        self.sel[...] = jnp.zeros_like(self.sel)
        for c in self.copies(0):
            c.start()

    def step(self, n):
        kind, q = self.steps[n]
        if n + 1 < len(self.steps):
            for c in self.copies(n + 1):
                c.start()
        row = lax.broadcasted_iota(jnp.int32, (128, self.slots), 0)
        if kind == 2:
            row = 2 * (row % 64) + row // 64
        for e in range(2):
            hit = self.ids[kind][2 * q + e : 2 * q + e + 1, :] == row
            self.sel[128 * e : 128 * e + 128, 128 * e : 128 * e + self.slots] = jnp.where(hit, 1.0, 0.0).astype(BF)
        for c in self.copies(n):
            c.wait()
        if kind < 2:
            self.place_in(n % 2, (kind * self.pairs + q) * 128)
        else:
            self.place_down(n % 2, q)

    def picked(self, slot, c):
        lanes = pl.ds(pl.multiple_of(c * 256, 256), 256)
        return jnp.dot(self.sel[...], self.raw[slot, :, lanes], preferred_element_type=F32)

    def place_in(self, slot, column):
        low = low_half(128)

        def body(c, carry):
            s = self.picked(slot, c)
            for k in range(2):
                a = s[:128, 128 * k : 128 * k + 128]
                b = swap(s[128:, 128 * k : 128 * k + 128])
                at = pl.ds(pl.multiple_of((2 * c + k) * 16, 16), 16)
                for p, v in enumerate((jnp.where(low, a, b), jnp.where(low, b, a))):
                    self.in_w[p, :, at, column : column + 128] = v.astype(BF).reshape(8, 16, 128)
            return carry

        lax.fori_loop(0, 16, body, 0, unroll=16)

    def place_down(self, slot, q):
        low = low_half(64)

        def body(c, carry):
            s = self.picked(slot, c)
            for k in range(2):
                for e in range(2):
                    a = s[128 * e : 128 * e + 64, 128 * k : 128 * k + 128]
                    b = s[128 * e + 64 : 128 * e + 128, 128 * k : 128 * k + 128]
                    at = pl.ds(2 * c + k, 64, stride=STRIDE)
                    self.turn[2 * e, at, :] = jnp.where(low, a, swap(b))
                    self.turn[2 * e + 1, at, :] = jnp.where(low, swap(a), b)
            return carry

        lax.fori_loop(0, 16, body, 0, unroll=16)

        def back(b, carry):
            for e in range(2):
                for p in range(2):
                    first = p * 64 * self.pairs + (2 * q + e) * 32
                    lanes = pl.ds(pl.multiple_of(128 * b, 128), 128)
                    at = pl.ds(pl.multiple_of(STRIDE * b, 8), 32)
                    self.down_w[first : first + 32, lanes] = self.turn[2 * e + p, at, :].astype(BF)
            return carry

        lax.fori_loop(0, 64, back, 0, unroll=64)


def gather_product(x_ref, in_w, acc, w, first):
    for p in range(2):
        term = jnp.dot(x_ref[w, :, 512 * p : 512 * p + 512], in_w[p, w], preferred_element_type=F32)
        if first:
            acc[p] = term
        else:
            acc[p] += term


def hidden_of(acc, half):
    cols = []
    for t in range(2 * half // 128):
        at = slice(128 * t, 128 * t + 128)
        cols.append(acc[0, :, at] + swap(acc[1, :, at]))
    count = half // 128
    out = [(jax.nn.silu(cols[t]) * cols[count + t]).astype(BF) for t in range(count)]
    h = jnp.concatenate(out, axis=1)
    quarter = half // 2

    def source(d):
        return (d % quarter) // 32 * 64 + 2 * (d % 32) + d // quarter

    return jnp.dot(h, one_hot(half, half, source), preferred_element_type=F32).astype(BF)


def fused_kernel(
    tok, gain, gi, ui, di, gb, ub, db, out,
    raw, sel, turn, in_w, down_w, acc, x, ssum, q, own, send0, land0, send1, land1, send2, land2, send3, land3,
    sems, ss_s, ss_r, z_s, z_r, a_s, a_r, b_s, b_r, c_s, c_r, r0_s, r0_r, r1_s, r1_r, r2_s, r2_r, r3_s, r3_r,
):
    wide, narrow = lax.axis_index("wide"), lax.axis_index("narrow")
    z, core = wide // 2, wide % 2
    y, xx = narrow // 2, narrow % 2
    sibling = {"wide": 2 * z + 1 - core}
    beside = ({"narrow": 2 * y + 1 - xx}, {"narrow": 2 * (1 - y) + xx})
    mine, other = (xx, y), (1 - xx, 1 - y)

    def plane(d):
        return (z + d) % 4

    def rows(h, pair, half, count):
        return pl.ds(pl.multiple_of(128 * h + 64 * pair + 32 * half, 32), count)

    def remote(src, dst, s, r, to):
        return pltpu.make_async_remote_copy(
            src_ref=src, dst_ref=dst, send_sem=s, recv_sem=r, device_id=to, device_id_type=pl.DeviceIdType.MESH
        )

    def own_rows(h):
        return rows(h, mine[1 - h], mine[h], 32)

    values = tok[...].astype(F32)
    ssum[0] = jnp.broadcast_to(jnp.sum(values * values, axis=-1, keepdims=True), ssum.shape[1:])

    barrier = pltpu.get_barrier_semaphore()
    peers = [{"wide": (wide + d) % 8} for d in range(1, 8)] + list(beside)
    for peer in peers:
        pl.semaphore_signal(barrier, inc=1, device_id=peer, device_id_type=pl.DeviceIdType.MESH)
    pl.semaphore_wait(barrier, len(peers))

    sums = [remote(ssum.at[0], ssum.at[d], ss_s.at[d], ss_r.at[d], peers[d - 1]) for d in range(1, 8)]
    for c in sums:
        c.start()

    panels = Panels((gb, ub, db), (gi, ui, di), raw, sel, turn, in_w, down_w, sems)
    panels.begin()
    panels.step(0)

    total = jnp.sum(values * values, axis=-1, keepdims=True)
    for d in range(1, 8):
        sums[d - 1].wait_recv()
        total = total + ssum[d, :, 0:1]
    inverse = lax.rsqrt(total / 8192.0 + 1e-05)
    normed = (values * inverse * gain[...].astype(F32)).astype(BF)
    for t in range(8):

        def source(d):
            d = d + 128 * t
            return (d % 16) * 64 + 2 * ((d % 512) // 16) + d // 512

        part = jnp.dot(normed, one_hot(1024, 128, source), preferred_element_type=F32).astype(BF)
        for h in range(2):
            x[wide, own_rows(h), 128 * t : 128 * t + 128] = part[32 * h : 32 * h + 32]

    def held(d):
        return 2 * plane(4 - d) + core

    along = {}
    first = {}
    second = {}
    last = {}
    for d in range(1, 4):
        for h in range(2):
            ref = x.at[wide, own_rows(h)]
            along[d, h] = remote(ref, ref, z_s.at[d, h], z_r.at[d, h], {"wide": 2 * plane(d) + core})
    for d in range(4):
        for h in range(2):
            ref = x.at[held(d), own_rows(h)]
            first[d, h] = remote(ref, ref, a_s.at[d, h], a_r.at[d, h], beside[h])
            ref = x.at[held(d), rows(h, mine[1 - h], 0, 64)]
            second[d, h] = remote(ref, ref, b_s.at[d, h], b_r.at[d, h], beside[1 - h])
        ref = x.at[held(d)]
        last[d] = remote(ref, ref, c_s.at[d], c_r.at[d], sibling)

    def go_first(d):
        for h in range(2):
            if d:
                along[d, h].wait_recv()
            first[d, h].start()

    def go_second(d):
        for h in range(2):
            first[d, h].wait_recv()
            second[d, h].start()

    def go_last(d):
        for h in range(2):
            second[d, h].wait_recv()
        last[d].start()

    for c in along.values():
        c.start()
    go_first(0)
    after = {
        3: [(go_first, 1), (go_second, 0)],
        5: [(go_first, 2), (go_first, 3)],
        7: [(go_second, 1), (go_last, 0)],
        8: [(go_second, 2), (go_last, 1)],
        9: [(go_second, 3), (go_last, 2)],
        10: [(go_last, 3)],
    }
    for n in range(1, len(panels.steps)):
        panels.step(n)
        for act, d in after.get(n, ()):
            act(d)

    for d in range(4):
        gather_product(x, in_w, acc, held(d), d == 0)
    for d in range(4):
        last[d].wait_recv()
        gather_product(x, in_w, acc, held(d) + 1 - 2 * core, False)
    hidden = hidden_of(acc, in_w.shape[3] // 2)

    def product(w):
        columns = pl.ds(pl.multiple_of(1024 * w, 1024), 1024)
        return jnp.dot(hidden, down_w[:, columns], preferred_element_type=F32)

    order = (1, 2, 3, 0)
    hop0, hop1, hop2, hop3 = {}, {}, {}, {}
    for e in order:
        hop0[e] = remote(send0.at[e], land0.at[e], r0_s.at[e], r0_r.at[e], sibling)
        for h in range(2):
            hop1[e, h] = remote(send1.at[e, h], land1.at[e, h], r1_s.at[e, h], r1_r.at[e, h], beside[1 - h])
            hop2[e, h] = remote(send2.at[e, h], land2.at[e, h], r2_s.at[e, h], r2_r.at[e, h], beside[h])
        if e:
            hop3[e] = remote(send3.at[e], land3.at[e], r3_s.at[e], r3_r.at[e], {"wide": 2 * plane(e) + core})
    for e in order:
        send0[e] = product(2 * plane(e) + 1 - core).astype(BF)
        hop0[e].start()
    for e in order:
        q[e] = product(2 * plane(e) + core)

    def go_hop1(e):
        hop0[e].wait_recv()
        for h in range(2):
            at = rows(h, other[1 - h], 0, 64)
            send1[e, h] = (q[e, at] + land0[e, at].astype(F32)).astype(BF)
            hop1[e, h].start()
        for h in range(2):
            at = rows(h, mine[1 - h], 0, 64)
            q[e, at] = q[e, at] + land0[e, at].astype(F32)

    def go_hop2(e):
        for h in range(2):
            hop1[e, h].wait_recv()
            at = rows(h, mine[1 - h], other[h], 32)
            come = pl.ds(pl.multiple_of(32 * other[h], 32), 32)
            send2[e, h] = (q[e, at] + land1[e, h, come].astype(F32)).astype(BF)
            hop2[e, h].start()

    def go_hop3(e):
        for h in range(2):
            hop2[e, h].wait_recv()
            come = pl.ds(pl.multiple_of(32 * mine[h], 32), 32)
            v = q[e, own_rows(h)] + land1[e, h, come].astype(F32) + land2[e, h].astype(F32)
            if e:
                send3[e, 32 * h : 32 * h + 32] = v.astype(BF)
            else:
                own[32 * h : 32 * h + 32] = v
        if e:
            hop3[e].start()

    for k in range(6):
        for lag, act in enumerate((go_hop1, go_hop2, go_hop3)):
            if 0 <= k - lag < 4:
                act(order[k - lag])
    value = own[...]
    for e in (1, 2, 3):
        hop3[e].wait_recv()
        value = value + land3[e].astype(F32)
    out[...] = value.astype(BF)

    for group in (along, first, second, last, hop0, hop1, hop2, hop3):
        for c in group.values():
            c.wait_send()
    for c in sums:
        c.wait_send()


def fused(tokens, norm_gain, gate_blocks, gate_ids, up_blocks, up_ids, down_blocks, down_ids):
    rows, width = tokens.shape
    count = gate_blocks.shape[0]
    vmem = pl.BlockSpec(memory_space=pltpu.VMEM)
    dma = pltpu.SemaphoreType.DMA
    return pl.pallas_call(
        fused_kernel,
        out_shape=jax.ShapeDtypeStruct(tokens.shape, BF),
        in_specs=[vmem] * 5 + [pl.BlockSpec(memory_space=pl.ANY)] * 3,
        out_specs=vmem,
        scratch_shapes=[
            pltpu.VMEM((2, 256, 4096), BF),
            pltpu.VMEM((256, 256), BF),
            pltpu.VMEM((4, 64 * STRIDE, 128), F32),
            pltpu.VMEM((2, 8, 512, 128 * count), BF),
            pltpu.VMEM((64 * count, 8192), BF),
            pltpu.VMEM((2, 256, 128 * count), F32),
            pltpu.VMEM((8, 256, 1024), BF),
            pltpu.VMEM((8, 64, 128), F32),
            pltpu.VMEM((4, 256, 1024), F32),
            pltpu.VMEM((64, 1024), F32),
            pltpu.VMEM((4, 256, 1024), BF),
            pltpu.VMEM((4, 256, 1024), BF),
            pltpu.VMEM((4, 2, 64, 1024), BF),
            pltpu.VMEM((4, 2, 64, 1024), BF),
            pltpu.VMEM((4, 2, 32, 1024), BF),
            pltpu.VMEM((4, 2, 32, 1024), BF),
            pltpu.VMEM((4, 64, 1024), BF),
            pltpu.VMEM((4, 64, 1024), BF),
            dma((2, 2)),
            dma((8,)), dma((8,)),
            dma((4, 2)), dma((4, 2)),
            dma((4, 2)), dma((4, 2)),
            dma((4, 2)), dma((4, 2)),
            dma((4,)), dma((4,)),
            dma((4,)), dma((4,)),
            dma((4, 2)), dma((4, 2)),
            dma((4, 2)), dma((4, 2)),
            dma((4,)), dma((4,)),
        ],
        compiler_params=pltpu.CompilerParams(
            vmem_limit_bytes=62 * 1024 * 1024, collective_id=0, has_side_effects=True
        ),
    )(tokens, norm_gain.reshape(1, width), gate_ids, up_ids, down_ids, gate_blocks, up_blocks, down_blocks)


def solution(mesh):
    placed = (
        P(("groups", "narrow"), "wide"),
        P("wide"),
        P(("wide", "narrow"), None, None),
        P(("wide", "narrow"), None),
        P(("wide", "narrow"), None, None),
        P(("wide", "narrow"), None),
        P(("wide", "narrow"), None, None),
        P(("wide", "narrow"), None),
    )
    local = fused if mesh.shape["wide"] == 8 and mesh.shape["narrow"] == 4 else plain
    return jax.shard_map(
        local,
        mesh=mesh,
        in_specs=placed,
        out_specs=P(("groups", "narrow"), "wide"),
        check_vma=False,
    )
```

```python
import functools

import jax
import jax.numpy as jnp
from jax import lax
from jax.experimental import pallas as pl
from jax.experimental.pallas import tpu as pltpu
from jax.sharding import PartitionSpec as P

BLOCK = 64
STRIDE = 40
BF = jnp.bfloat16
F32 = jnp.float32


def normalize(gathered, gain_all):
    values = gathered.astype(jnp.float32)
    inverse_rms = lax.rsqrt(jnp.mean(values * values, axis=-1, keepdims=True) + 1e-05)
    return (values * inverse_rms * gain_all.astype(jnp.float32)).astype(jnp.bfloat16)


def project_in(normed, part, block_list):
    row_count, width_total = normed.shape
    count_blocks, slot_count = block_list.shape
    pieces = normed.reshape(row_count, width_total // BLOCK, BLOCK)
    picked = jnp.take(pieces, jnp.maximum(block_list, 0).reshape(-1), axis=1)
    picked = picked.reshape(row_count, count_blocks, slot_count, BLOCK)
    tiles = jnp.where((block_list >= 0)[:, :, None], part, jnp.zeros_like(part))
    tiles = tiles.reshape(count_blocks, slot_count, BLOCK, BLOCK)
    result = jnp.einsum("rfkc,fkcj->rfj", picked, tiles, preferred_element_type=jnp.float32)
    return result.reshape(row_count, count_blocks * BLOCK)


def dense_down(part, block_list, width_total):
    count_blocks, slot_count = block_list.shape
    width_blocks = width_total // BLOCK
    selector = jax.nn.one_hot(block_list, width_blocks, dtype=jnp.bfloat16)
    tiles = part.reshape(count_blocks, slot_count, BLOCK, BLOCK)
    placed = jnp.einsum("fkb,fkij->fibj", selector, tiles, preferred_element_type=jnp.bfloat16)
    return placed.reshape(count_blocks * BLOCK, width_total)


def gated_hidden(normed, gate_part, gate_list, up_part, up_list):
    gate_value = project_in(normed, gate_part, gate_list)
    upward = project_in(normed, up_part, up_list)
    return (jax.nn.silu(gate_value) * upward).astype(jnp.bfloat16)


def plain(tokens, norm_gain, gate_blocks, gate_ids, up_blocks, up_ids, down_blocks, down_ids):
    gathered, gain_all = (
        lax.all_gather(tokens, "wide", axis=1, tiled=True),
        lax.all_gather(norm_gain, "wide", axis=0, tiled=True),
    )
    normed = normalize(gathered, gain_all)
    group_normed = lax.all_gather(normed, "narrow", axis=0, tiled=True)
    local_hidden = gated_hidden(group_normed, gate_blocks, gate_ids, up_blocks, up_ids)
    hidden = lax.all_to_all(local_hidden, "narrow", split_axis=0, concat_axis=1, tiled=True)
    down_all, down_list = (
        lax.all_gather(down_blocks, "narrow", axis=0, tiled=True),
        lax.all_gather(down_ids, "narrow", axis=0, tiled=True),
    )
    panel_dense = dense_down(down_all, down_list, gathered.shape[1])
    partial_value = jnp.dot(hidden, panel_dense, preferred_element_type=jnp.float32)
    return lax.psum_scatter(partial_value, "wide", scatter_dimension=1, tiled=True).astype(
        jnp.bfloat16
    )


def one_hot(rows, columns, source_of):
    r = lax.broadcasted_iota(jnp.int32, (rows, columns), 0)
    d = lax.broadcasted_iota(jnp.int32, (rows, columns), 1)
    return jnp.where(r == source_of(d), 1.0, 0.0).astype(BF)


def low_half(rows):
    return lax.broadcasted_iota(jnp.int32, (rows, 128), 1) < 64


def swap(x):
    return pltpu.roll(x, 64, 1)


class Panels:
    def __init__(self, blocks, ids, raw, sel, turn, in_w, down_w, sems):
        self.blocks, self.ids, self.raw, self.sel, self.turn = blocks, ids, raw, sel, turn
        self.in_w, self.down_w, self.sems = in_w, down_w, sems
        self.pairs = blocks[0].shape[0] // 2
        self.slots = blocks[0].shape[1]
        self.steps = [(k, q) for k in range(3) for q in range(self.pairs)]

    def copies(self, n):
        kind, q = self.steps[n]
        return [
            pltpu.make_async_copy(
                self.blocks[kind].at[2 * q + e],
                self.raw.at[n % 2, pl.ds(128 * e, self.slots)],
                self.sems.at[n % 2, e],
            )
            for e in range(2)
        ]

    def begin(self):
        self.raw[...] = jnp.zeros_like(self.raw)
        self.sel[...] = jnp.zeros_like(self.sel)
        for c in self.copies(0):
            c.start()

    def step(self, n):
        kind, q = self.steps[n]
        if n + 1 < len(self.steps):
            for c in self.copies(n + 1):
                c.start()
        row = lax.broadcasted_iota(jnp.int32, (128, self.slots), 0)
        if kind == 2:
            row = 2 * (row % 64) + row // 64
        for e in range(2):
            hit = self.ids[kind][2 * q + e : 2 * q + e + 1, :] == row
            self.sel[128 * e : 128 * e + 128, 128 * e : 128 * e + self.slots] = jnp.where(hit, 1.0, 0.0).astype(BF)
        for c in self.copies(n):
            c.wait()
        if kind < 2:
            self.place_in(n % 2, (kind * self.pairs + q) * 128)
        else:
            self.place_down(n % 2, q)

    def picked(self, slot, c):
        lanes = pl.ds(pl.multiple_of(c * 256, 256), 256)
        return jnp.dot(self.sel[...], self.raw[slot, :, lanes], preferred_element_type=F32)

    def place_in(self, slot, column):
        low = low_half(128)

        def body(c, carry):
            s = self.picked(slot, c)
            for k in range(2):
                a = s[:128, 128 * k : 128 * k + 128]
                b = swap(s[128:, 128 * k : 128 * k + 128])
                at = pl.ds(pl.multiple_of((2 * c + k) * 16, 16), 16)
                for p, v in enumerate((jnp.where(low, a, b), jnp.where(low, b, a))):
                    self.in_w[p, :, at, column : column + 128] = v.astype(BF).reshape(8, 16, 128)
            return carry

        lax.fori_loop(0, 16, body, 0, unroll=16)

    def place_down(self, slot, q):
        low = low_half(64)

        def body(c, carry):
            s = self.picked(slot, c)
            for k in range(2):
                for e in range(2):
                    a = s[128 * e : 128 * e + 64, 128 * k : 128 * k + 128]
                    b = s[128 * e + 64 : 128 * e + 128, 128 * k : 128 * k + 128]
                    at = pl.ds(2 * c + k, 64, stride=STRIDE)
                    self.turn[2 * e, at, :] = jnp.where(low, a, swap(b))
                    self.turn[2 * e + 1, at, :] = jnp.where(low, swap(a), b)
            return carry

        lax.fori_loop(0, 16, body, 0, unroll=16)

        def back(b, carry):
            for e in range(2):
                for p in range(2):
                    first = p * 64 * self.pairs + (2 * q + e) * 32
                    lanes = pl.ds(pl.multiple_of(128 * b, 128), 128)
                    at = pl.ds(pl.multiple_of(STRIDE * b, 8), 32)
                    self.down_w[first : first + 32, lanes] = self.turn[2 * e + p, at, :].astype(BF)
            return carry

        lax.fori_loop(0, 64, back, 0, unroll=64)


def gather_product(x_ref, in_w, acc, w, first):
    for p in range(2):
        term = jnp.dot(x_ref[w, :, 512 * p : 512 * p + 512], in_w[p, w], preferred_element_type=F32)
        if first:
            acc[p] = term
        else:
            acc[p] += term


def hidden_of(acc, half):
    cols = []
    for t in range(2 * half // 128):
        at = slice(128 * t, 128 * t + 128)
        cols.append(acc[0, :, at] + swap(acc[1, :, at]))
    count = half // 128
    out = [(jax.nn.silu(cols[t]) * cols[count + t]).astype(BF) for t in range(count)]
    h = jnp.concatenate(out, axis=1)
    quarter = half // 2

    def source(d):
        return (d % quarter) // 32 * 64 + 2 * (d % 32) + d // quarter

    return jnp.dot(h, one_hot(half, half, source), preferred_element_type=F32).astype(BF)


def fused_kernel(
    tok, gain, gi, ui, di, gb, ub, db, out,
    raw, sel, turn, in_w, down_w, acc, x, ssum, q, own, send0, land0, send1, land1, send2, land2, send3, land3,
    sems, ss_s, ss_r, z_s, z_r, a_s, a_r, b_s, b_r, c_s, c_r, r0_s, r0_r, r1_s, r1_r, r2_s, r2_r, r3_s, r3_r,
):
    wide, narrow = lax.axis_index("wide"), lax.axis_index("narrow")
    z, core = wide // 2, wide % 2
    y, xx = narrow // 2, narrow % 2
    sibling = {"wide": 2 * z + 1 - core}
    beside = ({"narrow": 2 * y + 1 - xx}, {"narrow": 2 * (1 - y) + xx})
    mine, other = (xx, y), (1 - xx, 1 - y)

    def plane(d):
        return (z + d) % 4

    def rows(h, pair, half, count):
        return pl.ds(pl.multiple_of(128 * h + 64 * pair + 32 * half, 32), count)

    def remote(src, dst, s, r, to):
        return pltpu.make_async_remote_copy(
            src_ref=src, dst_ref=dst, send_sem=s, recv_sem=r, device_id=to, device_id_type=pl.DeviceIdType.MESH
        )

    def own_rows(h):
        return rows(h, mine[1 - h], mine[h], 32)

    values = tok[...].astype(F32)
    ssum[0] = jnp.broadcast_to(jnp.sum(values * values, axis=-1, keepdims=True), ssum.shape[1:])

    barrier = pltpu.get_barrier_semaphore()
    peers = [{"wide": (wide + d) % 8} for d in range(1, 8)] + list(beside)
    for peer in peers:
        pl.semaphore_signal(barrier, inc=1, device_id=peer, device_id_type=pl.DeviceIdType.MESH)
    pl.semaphore_wait(barrier, len(peers))

    sums = [remote(ssum.at[0], ssum.at[d], ss_s.at[d], ss_r.at[d], peers[d - 1]) for d in range(1, 8)]
    for c in sums:
        c.start()

    panels = Panels((gb, ub, db), (gi, ui, di), raw, sel, turn, in_w, down_w, sems)
    panels.begin()
    panels.step(0)

    total = jnp.sum(values * values, axis=-1, keepdims=True)
    for d in range(1, 8):
        sums[d - 1].wait_recv()
        total = total + ssum[d, :, 0:1]
    inverse = lax.rsqrt(total / 8192.0 + 1e-05)
    normed = (values * inverse * gain[...].astype(F32)).astype(BF)
    for t in range(8):

        def source(d):
            d = d + 128 * t
            return (d % 16) * 64 + 2 * ((d % 512) // 16) + d // 512

        part = jnp.dot(normed, one_hot(1024, 128, source), preferred_element_type=F32).astype(BF)
        for h in range(2):
            x[wide, own_rows(h), 128 * t : 128 * t + 128] = part[32 * h : 32 * h + 32]

    def held(d):
        return 2 * plane(4 - d) + core

    along = {}
    first = {}
    second = {}
    last = {}
    for d in range(1, 4):
        for h in range(2):
            ref = x.at[wide, own_rows(h)]
            along[d, h] = remote(ref, ref, z_s.at[d, h], z_r.at[d, h], {"wide": 2 * plane(d) + core})
    for d in range(4):
        for h in range(2):
            ref = x.at[held(d), own_rows(h)]
            first[d, h] = remote(ref, ref, a_s.at[d, h], a_r.at[d, h], beside[h])
            ref = x.at[held(d), rows(h, mine[1 - h], 0, 64)]
            second[d, h] = remote(ref, ref, b_s.at[d, h], b_r.at[d, h], beside[1 - h])
        ref = x.at[held(d)]
        last[d] = remote(ref, ref, c_s.at[d], c_r.at[d], sibling)

    def go_first(d):
        for h in range(2):
            if d:
                along[d, h].wait_recv()
            first[d, h].start()

    def go_second(d):
        for h in range(2):
            first[d, h].wait_recv()
            second[d, h].start()

    def go_last(d):
        for h in range(2):
            second[d, h].wait_recv()
        last[d].start()

    for c in along.values():
        c.start()
    go_first(0)
    after = {
        3: [(go_first, 1), (go_second, 0)],
        5: [(go_first, 2), (go_first, 3)],
        7: [(go_second, 1), (go_last, 0)],
        8: [(go_second, 2), (go_last, 1)],
        9: [(go_second, 3), (go_last, 2)],
        10: [(go_last, 3)],
    }
    for n in range(1, len(panels.steps)):
        panels.step(n)
        for act, d in after.get(n, ()):
            act(d)

    for d in range(4):
        gather_product(x, in_w, acc, held(d), d == 0)
    for d in range(4):
        last[d].wait_recv()
        gather_product(x, in_w, acc, held(d) + 1 - 2 * core, False)
    hidden = hidden_of(acc, in_w.shape[3] // 2)

    def product(w):
        columns = pl.ds(pl.multiple_of(1024 * w, 1024), 1024)
        return jnp.dot(hidden, down_w[:, columns], preferred_element_type=F32)

    order = (1, 2, 3, 0)
    hop0, hop1, hop2, hop3 = {}, {}, {}, {}
    for e in order:
        hop0[e] = remote(send0.at[e], land0.at[e], r0_s.at[e], r0_r.at[e], sibling)
        for h in range(2):
            hop1[e, h] = remote(send1.at[e, h], land1.at[e, h], r1_s.at[e, h], r1_r.at[e, h], beside[1 - h])
            hop2[e, h] = remote(send2.at[e, h], land2.at[e, h], r2_s.at[e, h], r2_r.at[e, h], beside[h])
        if e:
            hop3[e] = remote(send3.at[e], land3.at[e], r3_s.at[e], r3_r.at[e], {"wide": 2 * plane(e) + core})
    for e in order:
        send0[e] = product(2 * plane(e) + 1 - core).astype(BF)
        hop0[e].start()

    def keep(e):
        q[e] = product(2 * plane(e) + core)

    def go_hop1(e):
        hop0[e].wait_recv()
        for h in range(2):
            at = rows(h, other[1 - h], 0, 64)
            send1[e, h] = (q[e, at] + land0[e, at].astype(F32)).astype(BF)
            hop1[e, h].start()
        for h in range(2):
            at = rows(h, mine[1 - h], 0, 64)
            q[e, at] = q[e, at] + land0[e, at].astype(F32)

    def go_hop2(e):
        for h in range(2):
            hop1[e, h].wait_recv()
            at = rows(h, mine[1 - h], other[h], 32)
            come = pl.ds(pl.multiple_of(32 * other[h], 32), 32)
            send2[e, h] = (q[e, at] + land1[e, h, come].astype(F32)).astype(BF)
            hop2[e, h].start()

    def go_hop3(e):
        for h in range(2):
            hop2[e, h].wait_recv()
            come = pl.ds(pl.multiple_of(32 * mine[h], 32), 32)
            v = q[e, own_rows(h)] + land1[e, h, come].astype(F32) + land2[e, h].astype(F32)
            if e:
                send3[e, 32 * h : 32 * h + 32] = v.astype(BF)
            else:
                own[32 * h : 32 * h + 32] = v
        if e:
            hop3[e].start()

    reduction = (
        (keep, 1), (keep, 2), (go_hop1, 1), (keep, 3), (go_hop1, 2), (keep, 0), (go_hop1, 3),
        (go_hop2, 1), (go_hop1, 0), (go_hop2, 2), (go_hop3, 1), (go_hop2, 3), (go_hop3, 2),
        (go_hop2, 0), (go_hop3, 3), (go_hop3, 0),
    )
    for act, e in reduction:
        act(e)
    value = own[...]
    for e in (1, 2, 3):
        hop3[e].wait_recv()
        value = value + land3[e].astype(F32)
    out[...] = value.astype(BF)

    for group in (along, first, second, last, hop0, hop1, hop2, hop3):
        for c in group.values():
            c.wait_send()
    for c in sums:
        c.wait_send()


def fused(tokens, norm_gain, gate_blocks, gate_ids, up_blocks, up_ids, down_blocks, down_ids):
    rows, width = tokens.shape
    count = gate_blocks.shape[0]
    vmem = pl.BlockSpec(memory_space=pltpu.VMEM)
    dma = pltpu.SemaphoreType.DMA
    return pl.pallas_call(
        fused_kernel,
        out_shape=jax.ShapeDtypeStruct(tokens.shape, BF),
        in_specs=[vmem] * 5 + [pl.BlockSpec(memory_space=pl.ANY)] * 3,
        out_specs=vmem,
        scratch_shapes=[
            pltpu.VMEM((2, 256, 4096), BF),
            pltpu.VMEM((256, 256), BF),
            pltpu.VMEM((4, 64 * STRIDE, 128), F32),
            pltpu.VMEM((2, 8, 512, 128 * count), BF),
            pltpu.VMEM((64 * count, 8192), BF),
            pltpu.VMEM((2, 256, 128 * count), F32),
            pltpu.VMEM((8, 256, 1024), BF),
            pltpu.VMEM((8, 64, 128), F32),
            pltpu.VMEM((4, 256, 1024), F32),
            pltpu.VMEM((64, 1024), F32),
            pltpu.VMEM((4, 256, 1024), BF),
            pltpu.VMEM((4, 256, 1024), BF),
            pltpu.VMEM((4, 2, 64, 1024), BF),
            pltpu.VMEM((4, 2, 64, 1024), BF),
            pltpu.VMEM((4, 2, 32, 1024), BF),
            pltpu.VMEM((4, 2, 32, 1024), BF),
            pltpu.VMEM((4, 64, 1024), BF),
            pltpu.VMEM((4, 64, 1024), BF),
            dma((2, 2)),
            dma((8,)), dma((8,)),
            dma((4, 2)), dma((4, 2)),
            dma((4, 2)), dma((4, 2)),
            dma((4, 2)), dma((4, 2)),
            dma((4,)), dma((4,)),
            dma((4,)), dma((4,)),
            dma((4, 2)), dma((4, 2)),
            dma((4, 2)), dma((4, 2)),
            dma((4,)), dma((4,)),
        ],
        compiler_params=pltpu.CompilerParams(
            vmem_limit_bytes=62 * 1024 * 1024, collective_id=0, has_side_effects=True
        ),
    )(tokens, norm_gain.reshape(1, width), gate_ids, up_ids, down_ids, gate_blocks, up_blocks, down_blocks)


def solution(mesh):
    placed = (
        P(("groups", "narrow"), "wide"),
        P("wide"),
        P(("wide", "narrow"), None, None),
        P(("wide", "narrow"), None),
        P(("wide", "narrow"), None, None),
        P(("wide", "narrow"), None),
        P(("wide", "narrow"), None, None),
        P(("wide", "narrow"), None),
    )
    local = fused if mesh.shape["wide"] == 8 and mesh.shape["narrow"] == 4 else plain
    return jax.shard_map(
        local,
        mesh=mesh,
        in_specs=placed,
        out_specs=P(("groups", "narrow"), "wide"),
        check_vma=False,
    )
```
